512 devices in a mesh: ep: 128 (over y, z, core), et: 4 (over x).
Axes of the slice: x: 4, y: 8, z: 8, core: 2. Of those that a mesh axis runs over, the one named last changes fastest.
Arguments:
- activations: bfloat16 [16384, 2048], P('ep', 'et'), may hold values from -6 to 6
- cotangent: bfloat16 [16384, 2048], P('ep', 'et'), may hold values from -6 to 6
- expert_ids: int32 [16384, 4], P('ep'), may hold values from 0 to 63, all different within a row; in each aligned block of 128 rows (0 to 127, 128 to 255, ...) at most 10 rows name the same one
- route_probs: bfloat16 [16384, 4], P('ep'), may hold values from 0.049804688 to 0.5
- gate_weight: bfloat16 [128, 704, 2048], P('ep', 'et'), may hold values from -0.125 to 0.125
- up_weight: bfloat16 [128, 704, 2048], P('ep', 'et'), may hold values from -0.125 to 0.125
- down_weight: bfloat16 [128, 704, 2048], P('ep', 'et'), may hold values from -0.15625 to 0.15625
Outputs:
- input_grad: bfloat16 [16384, 2048], P('ep', 'et')
- prob_grad: float32 [16384, 4], P('ep')
- gate_grad: bfloat16 [128, 704, 2048], P('ep', 'et')
- up_grad: bfloat16 [128, 704, 2048], P('ep', 'et')
- down_grad: bfloat16 [128, 704, 2048], P('ep', 'et')
The draws below stay inside these ranges and needn't reach their ends.
Inputs may be any that keep to these rules, and one draw needn't show every extreme that they name: `expert_ids`: each token names 4 different experts. Among the 128 tokens of one index of ep (aligned blocks of rows), no expert is named by more than 10 tokens, and in some blocks one expert is named by exactly 10.
All inputs are finite; a program needn't handle non-finite values.
Results may differ from the reference program's by a relative error of at most 0.017.
Values may be sent and summed in bfloat16 or wider, within the bound.
No kernel may reach another device: no remote copies, remote signals or barrier semaphores. Data moves between devices by JAX's collectives and lax.ppermute only.
A program may use at most 128 MiB of HBM per device.

```python
import math
import jax
import jax.numpy as jnp
import numpy as np
from jax import lax

D = 2048
FF = 1408
TOP = 4
TOK_DEV = 128
EXPERTS = 64
TOKENS = 16384
CAP = 10
N_EP = 128
N_ET = 4


def block_levels(stream_key, shape, pieces, least, top_value):
    def one(dim, parts):
        heights = jax.random.uniform(jax.random.fold_in(jax.random.fold_in(stream_key, 6), dim), (parts,), jnp.float32, least / len(pieces), top_value / len(pieces))
        return jnp.repeat(jnp.exp(heights), shape[dim] // parts).reshape((-1,) + (1,) * (len(shape) - dim - 1))

    gain = one(*pieces[0])
    for cut in pieces[1:]:
        gain = gain * one(*cut)
    return gain


def routed_block(key, own, number, rows, amount, top, limit, skew):
    order = jax.random.permutation(key, amount)
    heavy_load, ordinary = portions_of(amount, rows * top, limit, skew, True), portions_of(amount, rows * top, limit, skew, False)
    places = jnp.arange(amount)

    def named(tallies, rotation):
        used = int((tallies > 0).sum())
        fixed = max(1, used // 4)
        moved = fixed + (places - fixed + rotation * (used - fixed)) % max(1, amount - fixed)
        return jnp.zeros((amount,), jnp.int32).at[order[jnp.where(places < fixed, places, moved)]].set(jnp.asarray(tallies, jnp.int32))

    tallies = jnp.where(number % 4 == 0, named(heavy_load, number // 4), named(ordinary, number - number // 4 - 1))
    mixed = jax.random.permutation(jax.random.fold_in(own, 3), amount)
    source_of, taker = mixed[0:amount // 2 * 2:2], mixed[1:amount // 2 * 2:2]
    room = jnp.minimum(tallies[source_of] - 1, limit - tallies[taker]) // 2
    room = jnp.where((source_of == order[0]) | (taker == order[0]) | (tallies[taker] == 0), 0, jnp.maximum(room, 0))
    moved = jax.random.randint(jax.random.fold_in(own, 4), (amount // 2,), 0, 1 << 20) % (room + 1)
    tallies = tallies.at[source_of].add(-moved).at[taker].add(moved)
    members = jnp.searchsorted(jnp.cumsum(tallies), jnp.arange(rows * top), side="right").astype(jnp.int32)
    grid = members.reshape(top, rows).T
    grid = grid[jax.random.permutation(jax.random.fold_in(own, 1), rows)]
    rotation = jax.random.randint(jax.random.fold_in(own, 2), (rows, 1), 0, top)
    return jnp.take_along_axis(grid, (jnp.arange(top)[None, :] + rotation) % top, axis=1)


def portions_of(number_of, total, most, slope, full):
    portions = [(1 << 20) // math.isqrt(rank ** slope) + 1 for rank in range(1, number_of + 1)]
    largest = most if full else min(most, max(-(-total // number_of), total * portions[0] // sum(portions)))
    least = 1 if total - largest >= number_of - 1 else 0
    holding, rest = [largest] + [least] * (number_of - 1), total - largest - least * (number_of - 1)
    while rest > 0:
        free = [i for i in range(1, number_of) if holding[i] < largest] or [i for i in range(1, number_of) if holding[i] < most]
        mass, budget = sum([portions[i] for i in free]), rest
        for i in free:
            extra = min(most - holding[i], max(1, budget * portions[i] // mass), rest)
            holding[i] = holding[i] + extra
            rest = rest - extra
    return np.array(holding)


def bell_draw(rng, extent, deviation, limit, pieces=(), held_as=jnp.bfloat16):
    result = jax.random.normal(rng, extent, jnp.float32) * deviation
    if len(pieces) > 0:
        result = block_levels(rng, extent, pieces, -0.22, 0.18) * result
    return jnp.clip(result, min=-limit, max=limit).astype(held_as)


def setup_inputs(seed: int = 0) -> dict:
    seeds = jax.random.split(jax.random.key(seed), 8)
    activations = bell_draw(seeds[0], (TOKENS, D), 1.0, 6.0, ((0, 128), (1, 4)))
    cotangent = bell_draw(seeds[1], (TOKENS, D), 1.0, 6.0, ((0, 128), (1, 4)))
    expert_ids_keys = jax.random.split(jax.random.fold_in(seeds[2], 1), TOKENS // TOK_DEV)
    expert_ids_turns = jax.random.permutation(jax.random.fold_in(seeds[2], 3), TOKENS // TOK_DEV)
    expert_ids = jax.vmap(lambda own, number: routed_block(jax.random.fold_in(seeds[2], 2), own, number, TOK_DEV, EXPERTS, TOP, CAP, 2))(expert_ids_keys, expert_ids_turns).reshape((TOKENS, TOP))
    route_probs = jnp.clip(0.049804688 + 0.4501953 * jax.random.uniform(seeds[3], (TOKENS, TOP), jnp.float32) ** block_levels(seeds[3], (TOKENS, TOP), ((0, 128),), -0.2, 0.2), 0.049804688, 0.5).astype(jnp.bfloat16)
    gate_weight = bell_draw(seeds[4], (N_EP, FF // 2, D), D ** -0.5, 0.125, ((0, 128), (1, 4)))
    up_weight = bell_draw(seeds[5], (N_EP, FF // 2, D), D ** -0.5, 0.125, ((0, 128), (1, 4)))
    down_weight = bell_draw(seeds[6], (N_EP, FF // 2, D), FF ** -0.5, 0.15625, ((0, 128), (1, 4)))
    return {"activations": activations, "cotangent": cotangent, "expert_ids": expert_ids, "route_probs": route_probs, "gate_weight": gate_weight, "up_weight": up_weight, "down_weight": down_weight}


def silu_parts(pre_gate):
    sigmoid = jax.nn.sigmoid(pre_gate)
    return pre_gate * sigmoid, sigmoid * (1.0 + pre_gate * (1.0 - sigmoid))


def reference(activations, cotangent, expert_ids, route_probs, gate_weight, up_weight, down_weight):
    flat_ids = expert_ids.reshape(-1)
    routes = flat_ids.shape[0]
    one_hot = (flat_ids[:, None] == jnp.arange(EXPERTS, dtype=jnp.int32)[None, :]).astype(jnp.int32)
    blocks = one_hot.reshape(N_EP, TOK_DEV * TOP, EXPERTS)
    before = (jnp.cumsum(blocks, axis=1, dtype=jnp.int32) - blocks).reshape(routes, EXPERTS)
    position = jnp.sum(before * one_hot, axis=1, dtype=jnp.int32)
    source = jnp.arange(routes, dtype=jnp.int32) // (TOK_DEV * TOP)
    slot_index = ((flat_ids * N_EP + source) * CAP + position).astype(jnp.int32)
    total_slots = EXPERTS * N_EP * CAP
    route_of = jnp.zeros((total_slots,), jnp.int32).at[slot_index].set(jnp.arange(routes, dtype=jnp.int32))
    filled = jnp.zeros((total_slots,), jnp.float32).at[slot_index].set(1.0)
    rows_each = N_EP * CAP
    unit_block = FF // (2 * N_ET)
    prob_flat = route_probs.reshape(-1)

    def expert_step(carry, inputs):
        input_acc, prob_acc = carry
        route_rows, live, gate_pair, up_pair, down_pair = inputs
        token_rows = route_rows // TOP
        live_bf = live.astype(jnp.bfloat16)
        x_rows = activations[token_rows] * live_bf[:, None]
        grad_rows = cotangent[token_rows] * live_bf[:, None]
        weight_rows = (prob_flat[route_rows] * live_bf).astype(jnp.float32)[:, None]
        gate_full = gate_pair.reshape(FF, D).T
        up_full = up_pair.reshape(FF, D).T
        down_full = down_pair.reshape(FF, D)
        pre_gate = jnp.dot(x_rows, gate_full, preferred_element_type=jnp.float32)
        pre_up = jnp.dot(x_rows, up_full, preferred_element_type=jnp.float32)
        silu_value, silu_slope = silu_parts(pre_gate)
        hidden = silu_value * pre_up
        scaled_hidden = (weight_rows * hidden).astype(jnp.bfloat16)
        down_back = lax.dot_general(grad_rows, down_full, (((1,), (1,)), ((), ())), preferred_element_type=jnp.float32)
        prob_part = jnp.sum(hidden * down_back, axis=1)
        hidden_back = weight_rows * down_back
        gate_back = (hidden_back * pre_up * silu_slope).astype(jnp.bfloat16)
        up_back = (hidden_back * silu_value).astype(jnp.bfloat16)
        gate_g = jnp.dot(gate_back.T, x_rows, preferred_element_type=jnp.float32).astype(jnp.bfloat16)
        up_g = jnp.dot(up_back.T, x_rows, preferred_element_type=jnp.float32).astype(jnp.bfloat16)
        down_g = jnp.dot(scaled_hidden.T, grad_rows, preferred_element_type=jnp.float32).astype(jnp.bfloat16)
        gate_blocks = gate_back.astype(jnp.float32).reshape(rows_each, 2 * N_ET, unit_block)
        up_blocks = up_back.astype(jnp.float32).reshape(rows_each, 2 * N_ET, unit_block)
        gate_mats = gate_full.astype(jnp.float32).reshape(D, 2 * N_ET, unit_block)
        up_mats = up_full.astype(jnp.float32).reshape(D, 2 * N_ET, unit_block)
        block_part = jnp.einsum("rkf,dkf->rkd", gate_blocks, gate_mats) + jnp.einsum("rkf,dkf->rkd", up_blocks, up_mats)
        block_part = block_part.astype(jnp.bfloat16).astype(jnp.float32).reshape(rows_each, 2, N_ET, D)
        pair_part = (block_part[:, 0] + block_part[:, 1]).astype(jnp.bfloat16).astype(jnp.float32)
        route_grad = jnp.sum(pair_part, axis=1)
        input_acc = input_acc.at[token_rows].add(route_grad * live[:, None])
        prob_acc = prob_acc.at[route_rows].add(prob_part * live)
        return (input_acc, prob_acc), (gate_g, up_g, down_g)

    inputs = (route_of.reshape(EXPERTS, rows_each), filled.reshape(EXPERTS, rows_each),
              gate_weight.reshape(EXPERTS, 2, FF // 2, D), up_weight.reshape(EXPERTS, 2, FF // 2, D),
              down_weight.reshape(EXPERTS, 2, FF // 2, D))
    start = (jnp.zeros((TOKENS, D), jnp.float32), jnp.zeros((routes,), jnp.float32))
    (input_acc, prob_acc), (gate_all, up_all, down_all) = lax.scan(expert_step, start, inputs)
    gate_grad = gate_all.reshape(N_EP, FF // 2, D)
    up_grad = up_all.reshape(N_EP, FF // 2, D)
    down_grad = down_all.reshape(N_EP, FF // 2, D)
    return (input_acc.astype(jnp.bfloat16), prob_acc.reshape(TOKENS, TOP), gate_grad, up_grad, down_grad)
```

```python
import jax
import jax.numpy as jnp
from jax import lax
from jax.sharding import PartitionSpec as P

CAPACITY = 10
HEAD = 8
REST = CAPACITY - HEAD


def silu_parts(pre_gate):
    sigmoid = jax.nn.sigmoid(pre_gate)
    return (pre_gate * sigmoid, sigmoid * (1.0 + pre_gate * (1.0 - sigmoid)))


def dot_f32(left, right, left_dim, right_dim):
    return lax.dot_general(
        left, right, (((left_dim,), (right_dim,)), ((), ())), preferred_element_type=jnp.float32
    )


def same_core_groups(devices):
    return [list(range(core, devices, 2)) for core in range(2)]


def exchange_chips(block):
    return lax.all_to_all(
        block,
        "ep",
        split_axis=0,
        concat_axis=0,
        axis_index_groups=same_core_groups(lax.axis_size("ep")),
        tiled=True,
    )


def other_core(value):
    pairs = [(source, source ^ 1) for source in range(lax.axis_size("ep"))]
    return lax.ppermute(value, "ep", pairs)


def exchange_x(block):
    return lax.all_to_all(block, "et", split_axis=0, concat_axis=0, tiled=True)


def gather_x(block):
    count = lax.axis_size("et")
    copies = jnp.broadcast_to(block[None], (count,) + block.shape)
    parts = exchange_x(copies)
    return jnp.concatenate([parts[index] for index in range(count)], axis=1)


def two_halves(value):
    high = value.astype(jnp.bfloat16)
    low = (value - high.astype(jnp.float32)).astype(jnp.bfloat16)
    return high, low


def expand(values, experts, width):
    columns = jnp.arange(experts * width, dtype=jnp.int32) // width
    spread = (columns[None, :] == jnp.arange(experts, dtype=jnp.int32)[:, None]).astype(jnp.bfloat16)
    return dot_f32(values.astype(jnp.bfloat16), spread, 1, 0)


def shards(activations, cotangent, expert_ids, route_probs, gate_weight, up_weight, down_weight):
    tokens, quarter = activations.shape
    top_count = expert_ids.shape[1]
    experts = lax.axis_size("ep") // 2
    x_count = lax.axis_size("et")
    bf16 = jnp.bfloat16
    f32 = jnp.float32

    own_weights = jnp.concatenate([gate_weight[0], up_weight[0], down_weight[0]], axis=0)
    other_weights = other_core(own_weights)

    hits = expert_ids[:, :, None] == jnp.arange(experts, dtype=jnp.int32)[None, None, :]
    hit = jnp.sum(hits.astype(f32), axis=1)
    weight = jnp.sum(jnp.where(hits, route_probs.astype(f32)[:, :, None], 0.0), axis=1)
    row = jnp.arange(tokens, dtype=jnp.int32)
    earlier = (row[None, :] < row[:, None]).astype(bf16)
    rank = dot_f32(earlier, hit.astype(bf16), 1, 0)
    code = jnp.where(hit > 0.0, rank, 255.0)

    def selection(width, first):
        place = (jnp.arange(experts * width, dtype=jnp.int32) % width + first).astype(f32)
        return (expand(code, experts, width) == place[None, :]).astype(bf16)

    head_pick = selection(HEAD, 0)
    rest_pick = selection(REST, HEAD)
    head_weighted = head_pick * expand(weight, experts, HEAD).astype(bf16)
    rest_weighted = rest_pick * expand(weight, experts, REST).astype(bf16)
    head_send = jnp.concatenate(
        [
            dot_f32(head_pick, activations, 0, 0).astype(bf16),
            dot_f32(head_weighted, cotangent, 0, 0).astype(bf16),
        ],
        axis=1,
    )
    rest_send = jnp.concatenate(
        [
            dot_f32(rest_pick, activations, 0, 0).astype(bf16),
            dot_f32(rest_weighted, cotangent, 0, 0).astype(bf16),
        ],
        axis=1,
    )

    def fold_rest(block):
        folds = HEAD // REST
        lanes = block.shape[1] // folds
        shaped = block.reshape(experts, REST, folds, lanes).transpose(0, 2, 1, 3)
        return shaped.reshape(experts * HEAD, lanes)

    def unfold_rest(block):
        folds = HEAD // REST
        lanes = block.shape[1]
        shaped = block.reshape(experts, folds, REST, lanes).transpose(0, 2, 1, 3)
        return shaped.reshape(experts * REST, folds * lanes)

    send = jnp.concatenate([head_send, fold_rest(rest_send)], axis=1)
    got = exchange_chips(send.reshape(experts, HEAD, send.shape[1])).reshape(send.shape)
    got_rest = unfold_rest(got[:, 2 * quarter :])
    rows = jnp.concatenate([got[:, :quarter], got_rest[:, :quarter]], axis=0)
    grads = jnp.concatenate([got[:, quarter : 2 * quarter], got_rest[:, quarter:]], axis=0)
    full_rows = gather_x(rows)
    full_grads = gather_x(grads)
    slots = full_rows.shape[0]

    units = gate_weight.shape[1]
    wide = jnp.concatenate([own_weights[: 2 * units], other_weights[: 2 * units]], axis=0)
    down = jnp.concatenate([own_weights[2 * units :], other_weights[2 * units :]], axis=0)
    both_pre = dot_f32(full_rows, wide, 1, 1).reshape(slots, 2, 2, units)
    pre_gate = both_pre[:, :, 0].reshape(slots, 2 * units)
    pre_up = both_pre[:, :, 1].reshape(slots, 2 * units)
    silu_value, silu_slope = silu_parts(pre_gate)
    hidden = silu_value * pre_up
    down_back = dot_f32(full_grads, down, 1, 1)
    gate_back = (down_back * pre_up * silu_slope).astype(bf16)
    up_back = (down_back * silu_value).astype(bf16)
    prob_part = jnp.sum(hidden * down_back, axis=1)
    joint_back = jnp.concatenate(
        [gate_back[:, :units], up_back[:, :units], gate_back[:, units:], up_back[:, units:]], axis=1
    )
    block_part = dot_f32(joint_back, wide, 1, 0).astype(bf16)

    high, low = two_halves(prob_part)
    prob_rows = jnp.concatenate([high, low]).reshape(-1)
    prob_rows = jnp.pad(prob_rows, (0, 8 * quarter - prob_rows.shape[0])).reshape(8, quarter)
    parts = jnp.stack(
        [
            jnp.concatenate([block_part[:, i * quarter : (i + 1) * quarter], prob_rows], axis=0)
            for i in range(x_count)
        ]
    )
    summed = jnp.sum(exchange_x(parts).astype(f32), axis=0)
    route_grad = summed[:slots].astype(bf16)
    prob_flat = summed[slots:].reshape(-1)
    prob_sums = prob_flat[:slots] + prob_flat[slots : 2 * slots]
    prob_sums = jnp.concatenate(
        [
            prob_sums[: experts * HEAD].reshape(experts, HEAD),
            prob_sums[experts * HEAD :].reshape(experts, REST),
        ],
        axis=1,
    )
    sum_high, sum_low = two_halves(prob_sums)
    prob_tile = jnp.pad(
        jnp.stack([sum_high, sum_low], axis=1), ((0, 0), (0, HEAD - 2), (0, 128 - CAPACITY))
    ).reshape(experts * HEAD, 128)
    give = jnp.concatenate(
        [route_grad[: experts * HEAD], fold_rest(route_grad[experts * HEAD :]), prob_tile], axis=1
    )
    back = exchange_chips(give.reshape(experts, HEAD, give.shape[1])).reshape(give.shape)
    back_rest = unfold_rest(back[:, quarter : quarter + quarter * REST // HEAD])
    input_grad = (
        dot_f32(head_pick, back[:, :quarter], 1, 0) + dot_f32(rest_pick, back_rest, 1, 0)
    ).astype(bf16)
    back_probs = back[:, -128:].reshape(experts, HEAD, 128)[:, :2, :CAPACITY].astype(f32)
    back_probs = jnp.sum(back_probs, axis=1)
    by_expert = jnp.zeros((tokens, experts), f32)
    for place in range(CAPACITY):
        by_expert += jnp.where(code == place, back_probs[:, place][None, :], 0.0)
    prob_grad = jnp.sum(jnp.where(hits, by_expert[:, None, :], 0.0), axis=2)
    prob_grad = prob_grad / route_probs.astype(f32)

    wide_part = dot_f32(joint_back, full_rows, 0, 0)
    down_part = dot_f32(hidden.astype(bf16), full_grads, 0, 0)
    given = jnp.concatenate([wide_part[2 * units :], down_part[units:]], axis=0).astype(bf16)
    taken = other_core(given).astype(f32)
    gate_grad = (wide_part[:units] + taken[:units]).astype(bf16)[None]
    up_grad = (wide_part[units : 2 * units] + taken[units : 2 * units]).astype(bf16)[None]
    down_grad = (down_part[:units] + taken[2 * units :]).astype(bf16)[None]
    return (input_grad, prob_grad, gate_grad, up_grad, down_grad)


def solution(mesh):
    placed = (
        P("ep", "et"),
        P("ep", "et"),
        P("ep", None),
        P("ep", None),
        P("ep", "et", None),
        P("ep", "et", None),
        P("ep", "et", None),
    )
    return jax.shard_map(
        shards,
        mesh=mesh,
        in_specs=placed,
        out_specs=(
            P("ep", "et"),
            P("ep", None),
            P("ep", "et", None),
            P("ep", "et", None),
            P("ep", "et", None),
        ),
        check_vma=False,
    )
```

```python
import functools

import jax
import jax.numpy as jnp
from jax import lax
from jax.experimental import pallas as pl
from jax.experimental.pallas import tpu as pltpu
from jax.sharding import PartitionSpec as P

CAPACITY = 10
SHARE = CAPACITY // 2
HEAD = 4
TILE = 8
FOLDS = TILE // HEAD
LANES = 128
EXTRA = 16

bf16 = jnp.bfloat16
f32 = jnp.float32


def dot_f32(left, right, left_dim, right_dim):
    return lax.dot_general(
        left, right, (((left_dim,), (right_dim,)), ((), ())), preferred_element_type=f32
    )


def local_call(body, out_shape, *operands):
    return pl.pallas_call(
        body,
        out_shape=out_shape,
        compiler_params=pltpu.CompilerParams(vmem_limit_bytes=48 * 1024 * 1024),
    )(*operands)


def shape(rows, columns, dtype):
    return jax.ShapeDtypeStruct((rows, columns), dtype)


def iota(rows, columns, dim):
    return lax.broadcasted_iota(jnp.int32, (rows, columns), dim)


def exchange_chips(block):
    devices = lax.axis_size("ep")
    return lax.all_to_all(
        block,
        "ep",
        split_axis=0,
        concat_axis=0,
        axis_index_groups=[list(range(core, devices, 2)) for core in range(2)],
        tiled=True,
    )


def other_core(value):
    pairs = [(source, source ^ 1) for source in range(lax.axis_size("ep"))]
    return lax.ppermute(value, "ep", pairs)


def row_partner(value):
    count = lax.axis_size("et")
    return lax.ppermute(value, "et", [(source, count - 1 - source) for source in range(count)])


def unit_partner(value):
    pairs = [(source, source ^ 1) for source in range(lax.axis_size("et"))]
    return lax.ppermute(value, "et", pairs)


def is_upper():
    return lax.axis_index("et") >= 2


def is_outer():
    index = lax.axis_index("et")
    return (index == 0) | (index == 3)


def hit_of(ids, top, experts):
    return ids[:, top : top + 1] == iota(ids.shape[0], experts, 1)


def place_codes(ids, experts, upper):
    tokens, top_count = ids.shape
    hit = sum(hit_of(ids, top, experts).astype(f32) for top in range(top_count))
    earlier = (iota(tokens, tokens, 1) < iota(tokens, tokens, 0)).astype(f32).astype(bf16)
    rank = dot_f32(earlier, hit.astype(bf16), 1, 0)
    shift = jnp.where(upper, float(SHARE), 0.0)
    return jnp.where(hit > 0.0, rank - shift, 255.0)


def as_mask(condition):
    return jnp.where(condition, 1.0, 0.0)


def pack_kernel(ids_ref, probs_ref, own_x_ref, own_dy_ref, got_ref, send_ref):
    ids = ids_ref[...]
    tokens, top_count = ids.shape
    quarter = own_x_ref.shape[1]
    wide = send_ref.shape[0]
    experts = wide // TILE
    upper = is_upper()
    code = place_codes(ids, experts, upper)
    probs = probs_ref[...].astype(f32)
    weight = sum(
        jnp.where(hit_of(ids, top, experts), probs[:, top : top + 1], 0.0)
        for top in range(top_count)
    )
    spread = as_mask(iota(wide, experts, 0) // TILE == iota(wide, experts, 1)).astype(bf16)
    wide_code = dot_f32(spread, code.astype(bf16), 1, 1)
    wide_weight = dot_f32(spread, weight.astype(bf16), 1, 1)
    row = iota(wide, tokens, 0) % TILE
    head = wide_code == (row % HEAD).astype(f32)
    rest = wide_code == float(HEAD)
    edge = quarter + FOLDS * quarter // TILE

    def place(first, second, scale, start):
        main = jnp.zeros((wide, quarter), f32)
        tail = jnp.zeros((wide, LANES), f32)
        for fold, part in enumerate((first, second)):
            pick = jnp.where(head & (row // HEAD == fold), scale, 0.0).astype(bf16)
            main += dot_f32(pick, part, 1, 0)
            for index in range(HEAD):
                pick = jnp.where(rest & (row == fold * HEAD + index), scale, 0.0).astype(bf16)
                tail += dot_f32(pick, part[:, index * LANES : (index + 1) * LANES], 1, 0)
        send_ref[:, start : start + quarter] = main.astype(bf16)
        send_ref[:, start + quarter : start + edge] = tail.astype(bf16)

    own_x, own_dy = own_x_ref[...], own_dy_ref[...]
    got_x, got_dy = got_ref[:tokens], got_ref[tokens:]
    place(
        jnp.where(upper, got_x, own_x),
        jnp.where(upper, own_x, got_x),
        jnp.ones((wide, tokens), f32),
        0,
    )
    place(
        jnp.where(upper, got_dy, own_dy), jnp.where(upper, own_dy, got_dy), wide_weight, edge
    )


def unpack_kernel(mine_ref, theirs_ref, full_ref):
    wide = mine_ref.shape[0]
    quarter = full_ref.shape[1] // 4
    experts = wide // TILE
    heads = experts * HEAD
    outer = is_outer()
    mine, theirs = mine_ref[...], theirs_ref[...]
    slot = iota(heads, wide, 0)
    source = iota(heads, wide, 1)
    rest_slot = iota(experts, wide, 0)
    rest_source = iota(experts, wide, 1)
    places = ((0, 3), (1, 2))
    for side, columns in enumerate(places):
        block = jnp.where(outer, mine, theirs) if side == 0 else jnp.where(outer, theirs, mine)
        for fold, column in enumerate(columns):
            pick = as_mask(source == slot // HEAD * TILE + fold * HEAD + slot % HEAD).astype(bf16)
            full_ref[:heads, column * quarter : (column + 1) * quarter] = dot_f32(
                pick, block[:, :quarter], 1, 0
            ).astype(bf16)
            for index in range(HEAD):
                pick = as_mask(rest_source == rest_slot * TILE + fold * HEAD + index).astype(bf16)
                start = column * quarter + index * LANES
                full_ref[heads:, start : start + LANES] = dot_f32(
                    pick, block[:, quarter:], 1, 0
                ).astype(bf16)


def back_kernel(half, pre_ref, down_ref, joint_ref, hidden_ref, prob_ref):
    slots = pre_ref.shape[0]
    ones = jnp.ones((EXTRA, half), bf16)
    total = jnp.zeros((EXTRA, slots), f32)
    for part in range(2):
        start = 2 * half * part
        pre_gate = pre_ref[:, start : start + half]
        pre_up = pre_ref[:, start + half : start + 2 * half]
        down_back = down_ref[:, half * part : half * (part + 1)]
        sigmoid = jax.nn.sigmoid(pre_gate)
        silu_value = pre_gate * sigmoid
        hidden = silu_value * pre_up
        slope = sigmoid * (1.0 + pre_gate * (1.0 - sigmoid))
        joint_ref[:, start : start + half] = (down_back * pre_up * slope).astype(bf16)
        joint_ref[:, start + half : start + 2 * half] = (down_back * silu_value).astype(bf16)
        hidden_ref[:, half * part : half * (part + 1)] = hidden.astype(bf16)
        product = hidden * down_back
        high = product.astype(bf16)
        low = (product - high.astype(f32)).astype(bf16)
        total += dot_f32(ones, high, 1, 1) + dot_f32(ones, low, 1, 1)
    high = total.astype(bf16)
    low = (total - high.astype(f32)).astype(bf16)
    row = iota(EXTRA, slots, 0)
    zero = jnp.zeros_like(high)
    prob_ref[...] = jnp.zeros_like(prob_ref)
    prob_ref[:, :slots] = jnp.where(row == 0, high, jnp.where(row == 1, low, zero))


def give_kernel(block_ref, prob_ref, got_ref, give_ref):
    slots = block_ref.shape[0]
    quarter = block_ref.shape[1] // 4
    wide = give_ref.shape[0]
    experts = wide // TILE
    heads = experts * HEAD
    outer = is_outer()
    slot = iota(wide, heads, 1)
    target = iota(wide, heads, 0)
    rest_slot = iota(wide, experts, 1)
    rest_target = iota(wide, experts, 0)
    main = jnp.zeros((wide, quarter), f32)
    tail = jnp.zeros((wide, LANES), f32)
    for fold, (outside, inside) in enumerate(((0, 1), (3, 2))):
        kept = jnp.where(
            outer,
            block_ref[:, outside * quarter : (outside + 1) * quarter],
            block_ref[:, inside * quarter : (inside + 1) * quarter],
        )
        got = got_ref[:slots, fold * quarter : (fold + 1) * quarter]
        route = (kept.astype(f32) + got.astype(f32)).astype(bf16)
        pick = as_mask(target == slot // HEAD * TILE + fold * HEAD + slot % HEAD).astype(bf16)
        main += dot_f32(pick, route[:heads], 1, 0)
        for index in range(HEAD):
            pick = as_mask(rest_target == rest_slot * TILE + fold * HEAD + index).astype(bf16)
            tail += dot_f32(pick, route[heads:, index * LANES : (index + 1) * LANES], 1, 0)
    give_ref[:, :quarter] = main.astype(bf16)
    give_ref[:, quarter : quarter + LANES] = tail.astype(bf16)
    both = prob_ref[:, :slots].astype(f32) + got_ref[slots:, :slots].astype(f32)
    total = jnp.sum(both, axis=0, keepdims=True)
    high = total.astype(bf16).astype(f32)
    rows = iota(LANES, slots, 0)
    spread = jnp.where(rows == 0, high, jnp.where(rows == 1, total - high, 0.0)).astype(bf16)
    place = iota(wide, slots, 0)
    column = iota(wide, slots, 1)
    row = place % TILE
    expected = jnp.where(row < HEAD, place // TILE * HEAD + row, heads + place // TILE)
    pick = as_mask((column == expected) & (row < SHARE)).astype(bf16)
    give_ref[:, quarter + LANES :] = dot_f32(pick, spread, 1, 1).astype(bf16)


def combine_kernel(ids_ref, back_ref, own_ref, pass_ref):
    ids = ids_ref[...]
    tokens = ids.shape[0]
    quarter = own_ref.shape[1]
    wide = back_ref.shape[0]
    experts = wide // TILE
    upper = is_upper()
    code = place_codes(ids, experts, upper)
    spread = as_mask(iota(experts, wide, 0) == iota(experts, wide, 1) // TILE).astype(bf16)
    wide_code = dot_f32(code.astype(bf16), spread, 1, 0)
    row = iota(tokens, wide, 1) % TILE
    head = wide_code == (row % HEAD).astype(f32)
    rest = wide_code == float(HEAD)
    back_main = back_ref[:, :quarter]
    back_tail = back_ref[:, quarter : quarter + LANES]
    sums = []
    for fold in range(FOLDS):
        pick = as_mask(head & (row // HEAD == fold)).astype(bf16)
        tails = []
        for index in range(HEAD):
            tail_pick = as_mask(rest & (row == fold * HEAD + index)).astype(bf16)
            tails.append(dot_f32(tail_pick, back_tail, 1, 0))
        sums.append(dot_f32(pick, back_main, 1, 0) + jnp.concatenate(tails, axis=1))
    own_ref[...] = jnp.where(upper, sums[1], sums[0])
    pass_ref[:, :quarter] = jnp.where(upper, sums[0], sums[1]).astype(bf16)
    columns = back_ref[:, quarter + LANES :].astype(f32)
    lane = iota(wide, LANES, 1)
    expert = iota(wide, LANES, 0) // TILE
    by_lane = jnp.where(lane == expert, columns[:, 0:1], 0.0)
    by_lane += jnp.where(lane == expert + LANES // 2, columns[:, 1:2], 0.0)
    pick = as_mask(wide_code == row.astype(f32)).astype(bf16)
    pass_ref[:, quarter:] = dot_f32(pick, by_lane.astype(bf16), 1, 0).astype(bf16)


def finish_kernel(ids_ref, probs_ref, own_ref, pass_ref, got_ref, input_ref, prob_ref):
    ids = ids_ref[...]
    tokens, top_count = ids.shape
    quarter = own_ref.shape[1]
    input_ref[...] = (own_ref[...] + got_ref[:, :quarter].astype(f32)).astype(bf16)
    total = pass_ref[:, quarter:].astype(f32) + got_ref[:, quarter:].astype(f32)
    expert = iota(tokens, LANES, 1) % (LANES // 2)
    chosen = [
        jnp.sum(jnp.where(ids[:, top : top + 1] == expert, total, 0.0), axis=1, keepdims=True)
        for top in range(top_count)
    ]
    prob_ref[...] = jnp.concatenate(chosen, axis=1) / probs_ref[...].astype(f32)


def shards(activations, cotangent, expert_ids, route_probs, gate_weight, up_weight, down_weight):
    tokens, quarter = activations.shape
    experts = lax.axis_size("ep") // 2
    units = gate_weight.shape[1]
    wide = experts * TILE
    slots = experts * SHARE
    edge = quarter + LANES
    outer = is_outer()

    got_tokens = row_partner(jnp.concatenate([activations, cotangent], axis=0))
    own_weights = jnp.concatenate([gate_weight[0], up_weight[0], down_weight[0]], axis=0)
    got_tokens, own_weights = lax.optimization_barrier((got_tokens, own_weights))
    far_weights = row_partner(own_weights)
    own_twin = other_core(own_weights)
    far_twin = other_core(far_weights)

    send = local_call(
        pack_kernel,
        shape(wide, 2 * edge, bf16),
        expert_ids,
        route_probs,
        activations,
        cotangent,
        got_tokens,
    )
    got = exchange_chips(send.reshape(experts, TILE, 2 * edge))
    half = -(-2 * units // LANES) * LANES
    gap = jnp.zeros((half - 2 * units, 4 * quarter), bf16)

    def joined(index):
        part = slice(index * units, (index + 1) * units)
        return (
            [far_weights[part], far_twin[part], gap],
            [own_weights[part], own_twin[part], gap],
        )

    (far_gate, own_gate), (far_up, own_up), (far_down, own_down) = joined(0), joined(1), joined(2)
    wide_all = jnp.concatenate(far_gate + far_up + own_gate + own_up, axis=0)
    down_all = jnp.concatenate(far_down + own_down, axis=0)
    rows = got[:, :, :edge].reshape(wide, edge)
    grads = got[:, :, edge:].reshape(wide, edge)
    full = shape(slots, 4 * quarter, bf16)
    their_rows = unit_partner(rows)
    their_grads = unit_partner(grads)
    their_rows, wide_all, down_all = lax.optimization_barrier((their_rows, wide_all, down_all))
    full_rows = local_call(unpack_kernel, full, rows, their_rows)
    full_grads = local_call(unpack_kernel, full, grads, their_grads)
    pre = dot_f32(full_rows, wide_all, 1, 1)
    down_back = dot_f32(full_grads, down_all, 1, 1)
    joint, hidden, prob = local_call(
        functools.partial(back_kernel, half),
        (
            shape(slots, 4 * half, bf16),
            shape(slots, 2 * half, bf16),
            shape(EXTRA, 2 * quarter, bf16),
        ),
        pre,
        down_back,
    )
    block = dot_f32(joint, wide_all, 1, 0).astype(bf16)
    outside = jnp.concatenate([block[:, :quarter], block[:, 3 * quarter :]], axis=1)
    inside = block[:, quarter : 3 * quarter]
    given = jnp.concatenate([jnp.where(outer, inside, outside), prob], axis=0)
    taken = unit_partner(given)
    given, joint_late, hidden_late = lax.optimization_barrier((given, joint, hidden))

    def unit_grads(part):
        wide_part = dot_f32(joint_late[:, 2 * half * part : 2 * half * (part + 1)], full_rows, 0, 0)
        down_part = dot_f32(hidden_late[:, half * part : half * (part + 1)], full_grads, 0, 0)
        wide_part, down_part = wide_part.astype(bf16), down_part.astype(bf16)
        starts = ((wide_part, 0), (wide_part, half), (down_part, 0))
        kept = jnp.concatenate([a[s : s + units] for a, s in starts], axis=0)
        sent = jnp.concatenate([a[s + units : s + 2 * units] for a, s in starts], axis=0)
        return kept.astype(f32) + other_core(sent).astype(f32)

    far_grads = unit_grads(0).astype(bf16)
    far_got = row_partner(far_grads)
    taken, far_grads = lax.optimization_barrier((taken, far_grads))
    own_grads = (unit_grads(1) + far_got.astype(f32)).astype(bf16)

    give = local_call(give_kernel, shape(wide, edge + LANES, bf16), block, prob, taken)
    back = exchange_chips(give.reshape(experts, TILE, edge + LANES)).reshape(wide, edge + LANES)
    own_sum, passed = local_call(
        combine_kernel,
        (shape(tokens, quarter, f32), shape(tokens, quarter + LANES, bf16)),
        expert_ids,
        back,
    )
    input_grad, prob_grad = local_call(
        finish_kernel,
        (shape(tokens, quarter, bf16), shape(tokens, expert_ids.shape[1], f32)),
        expert_ids,
        route_probs,
        own_sum,
        passed,
        row_partner(passed),
    )
    return (
        input_grad,
        prob_grad,
        own_grads[:units][None],
        own_grads[units : 2 * units][None],
        own_grads[2 * units :][None],
    )


def solution(mesh):
    placed = (
        P("ep", "et"),
        P("ep", "et"),
        P("ep", None),
        P("ep", None),
        P("ep", "et", None),
        P("ep", "et", None),
        P("ep", "et", None),
    )
    return jax.shard_map(
        shards,
        mesh=mesh,
        in_specs=placed,
        out_specs=(
            P("ep", "et"),
            P("ep", None),
            P("ep", "et", None),
            P("ep", "et", None),
            P("ep", "et", None),
        ),
        check_vma=False,
    )
```

```python
import functools

import jax
import jax.numpy as jnp
from jax import lax
from jax.experimental import pallas as pl
from jax.experimental.pallas import tpu as pltpu
from jax.sharding import PartitionSpec as P

CAPACITY = 10
SHARE = CAPACITY // 2
HEAD = 4
TILE = 8
FOLDS = TILE // HEAD
LANES = 128
EXTRA = 16

bf16 = jnp.bfloat16
f32 = jnp.float32


def dot_f32(left, right, left_dim, right_dim):
    return lax.dot_general(
        left, right, (((left_dim,), (right_dim,)), ((), ())), preferred_element_type=f32
    )


def local_call(body, out_shape, *operands, mib=12, **options):
    return pl.pallas_call(
        body,
        out_shape=out_shape,
        cost_estimate=pl.CostEstimate(flops=0, bytes_accessed=0, transcendentals=0),
        compiler_params=pltpu.CompilerParams(vmem_limit_bytes=mib * 1024 * 1024),
        **options,
    )(*operands)


def shape(rows, columns, dtype):
    return jax.ShapeDtypeStruct((rows, columns), dtype)


def iota(rows, columns, dim):
    return lax.broadcasted_iota(jnp.int32, (rows, columns), dim)


def exchange_chips(block):
    devices = lax.axis_size("ep")
    return lax.all_to_all(
        block,
        "ep",
        split_axis=0,
        concat_axis=0,
        axis_index_groups=[list(range(core, devices, 2)) for core in range(2)],
        tiled=True,
    )


def other_core(value):
    pairs = [(source, source ^ 1) for source in range(lax.axis_size("ep"))]
    return lax.ppermute(value, "ep", pairs)


def row_partner(value):
    count = lax.axis_size("et")
    return lax.ppermute(value, "et", [(source, count - 1 - source) for source in range(count)])


def unit_partner(value):
    pairs = [(source, source ^ 1) for source in range(lax.axis_size("et"))]
    return lax.ppermute(value, "et", pairs)


def is_upper():
    return lax.axis_index("et") >= 2


def is_outer():
    index = lax.axis_index("et")
    return (index == 0) | (index == 3)


def hit_of(ids, top, experts):
    return ids[:, top : top + 1] == iota(ids.shape[0], experts, 1)


def place_codes(ids, experts, upper):
    tokens, top_count = ids.shape
    hit = sum(hit_of(ids, top, experts).astype(f32) for top in range(top_count))
    earlier = (iota(tokens, tokens, 1) < iota(tokens, tokens, 0)).astype(f32).astype(bf16)
    rank = dot_f32(earlier, hit.astype(bf16), 1, 0)
    shift = jnp.where(upper, float(SHARE), 0.0)
    return jnp.where(hit > 0.0, rank - shift, 255.0)


def as_mask(condition):
    return jnp.where(condition, 1.0, 0.0)


def pack_kernel(ids_ref, probs_ref, own_x_ref, own_dy_ref, got_ref, send_ref):
    ids = ids_ref[...]
    tokens, top_count = ids.shape
    quarter = own_x_ref.shape[1]
    wide = send_ref.shape[0]
    experts = wide // TILE
    upper = is_upper()
    code = place_codes(ids, experts, upper)
    probs = probs_ref[...].astype(f32)
    weight = sum(
        jnp.where(hit_of(ids, top, experts), probs[:, top : top + 1], 0.0)
        for top in range(top_count)
    )
    spread = as_mask(iota(wide, experts, 0) // TILE == iota(wide, experts, 1)).astype(bf16)
    wide_code = dot_f32(spread, code.astype(bf16), 1, 1)
    wide_weight = dot_f32(spread, weight.astype(bf16), 1, 1)
    row = iota(wide, tokens, 0) % TILE
    head = wide_code == (row % HEAD).astype(f32)
    rest = wide_code == float(HEAD)
    edge = quarter + FOLDS * quarter // TILE

    def place(first, second, scale, start):
        main = jnp.zeros((wide, quarter), f32)
        tail = jnp.zeros((wide, LANES), f32)
        for fold, part in enumerate((first, second)):
            pick = jnp.where(head & (row // HEAD == fold), scale, 0.0).astype(bf16)
            main += dot_f32(pick, part, 1, 0)
            for index in range(HEAD):
                pick = jnp.where(rest & (row == fold * HEAD + index), scale, 0.0).astype(bf16)
                tail += dot_f32(pick, part[:, index * LANES : (index + 1) * LANES], 1, 0)
        send_ref[:, start : start + quarter] = main.astype(bf16)
        send_ref[:, start + quarter : start + edge] = tail.astype(bf16)

    own_x, own_dy = own_x_ref[...], own_dy_ref[...]
    got_x, got_dy = got_ref[:tokens], got_ref[tokens:]
    place(
        jnp.where(upper, got_x, own_x),
        jnp.where(upper, own_x, got_x),
        jnp.ones((wide, tokens), f32),
        0,
    )
    place(
        jnp.where(upper, got_dy, own_dy), jnp.where(upper, own_dy, got_dy), wide_weight, edge
    )


def unpack(mine, theirs, outer, full_ref):
    wide = mine.shape[0]
    quarter = full_ref.shape[1] // 4
    experts = wide // TILE
    heads = experts * HEAD
    slot = iota(heads, wide, 0)
    source = iota(heads, wide, 1)
    rest_slot = iota(experts, wide, 0)
    rest_source = iota(experts, wide, 1)
    places = ((0, 3), (1, 2))
    for side, columns in enumerate(places):
        block = jnp.where(outer, mine, theirs) if side == 0 else jnp.where(outer, theirs, mine)
        for fold, column in enumerate(columns):
            pick = as_mask(source == slot // HEAD * TILE + fold * HEAD + slot % HEAD).astype(bf16)
            full_ref[:heads, column * quarter : (column + 1) * quarter] = dot_f32(
                pick, block[:, :quarter], 1, 0
            ).astype(bf16)
            for index in range(HEAD):
                pick = as_mask(rest_source == rest_slot * TILE + fold * HEAD + index).astype(bf16)
                start = column * quarter + index * LANES
                full_ref[heads:, start : start + LANES] = dot_f32(
                    pick, block[:, quarter:], 1, 0
                ).astype(bf16)


def load_units(sources, kind, units, target, sems):
    far, twin, own, own_twin = sources[0], sources[1 + kind], sources[4], sources[5]
    rows = pl.ds(kind * units, units)
    pieces = (far.at[rows], twin, own.at[rows], own_twin.at[rows])
    copies = []
    for place, piece in enumerate(pieces):
        copy = pltpu.make_async_copy(
            piece, target.at[pl.ds(place * units, units)], sems.at[kind * 4 + place]
        )
        copy.start()
        copies.append(copy)
    return copies


def wait_all(copies):
    for copy in copies:
        copy.wait()


def back_kernel(units, mine_ref, theirs_ref, *refs):
    sources = refs[:6]
    rows_ref, grads_ref, gate_ref, up_ref, sums_ref, given_ref = refs[6:12]
    parts = refs[12:24]
    w_gate, w_up, w_down, sems = refs[24:]
    gate_copies = load_units(sources, 0, units, w_gate, sems)
    up_copies = load_units(sources, 1, units, w_up, sems)
    down_copies = load_units(sources, 2, units, w_down, sems)
    outer = is_outer()
    slots = rows_ref.shape[0]
    edge = mine_ref.shape[1] // 2
    unpack(mine_ref[:, :edge], theirs_ref[:, :edge], outer, rows_ref)
    wait_all(gate_copies)
    pre_gate = dot_f32(rows_ref[...], w_gate[...], 1, 1)
    wait_all(up_copies)
    pre_up = dot_f32(rows_ref[...], w_up[...], 1, 1)
    unpack(mine_ref[:, edge:], theirs_ref[:, edge:], outer, grads_ref)
    wait_all(down_copies)
    down_back = dot_f32(grads_ref[...], w_down[...], 1, 1)
    sigmoid = jax.nn.sigmoid(pre_gate)
    silu_value = pre_gate * sigmoid
    hidden = silu_value * pre_up
    slope = sigmoid * (1.0 + pre_gate * (1.0 - sigmoid))
    gate_back = (down_back * pre_up * slope).astype(bf16)
    up_back = (down_back * silu_value).astype(bf16)
    hidden_bf = hidden.astype(bf16)
    gate_ref[...] = gate_back
    up_ref[...] = up_back
    for kind, value in enumerate((gate_back, up_back, hidden_bf)):
        for place in range(4):
            parts[3 * place + kind][...] = value[:, place * units : (place + 1) * units]
    product = hidden * down_back
    high = product.astype(bf16)
    low = (product - high.astype(f32)).astype(bf16)
    ones = jnp.ones((EXTRA, product.shape[1]), bf16)
    total = dot_f32(ones, high, 1, 1) + dot_f32(ones, low, 1, 1)
    high = total.astype(bf16).astype(f32)
    row = iota(EXTRA, slots, 0)
    sums = jnp.where(row == 0, high, jnp.where(row == 1, total - high, 0.0)).astype(bf16)
    sums_ref[...] = jnp.zeros_like(sums_ref)
    sums_ref[:, :slots] = sums
    given_ref[slots:, :] = jnp.zeros((EXTRA, given_ref.shape[1]), bf16)
    given_ref[slots:, :slots] = sums
    blocks(gate_ref, up_ref, w_gate, w_up, outer, ((1, 0), (2, 3)), given_ref, slots)


def blocks(gate_ref, up_ref, w_gate, w_up, outer, places, target, slots):
    quarter = target.shape[1] // FOLDS
    for fold, (outer_place, inner_place) in enumerate(places):
        place = jnp.where(outer, outer_place, inner_place)
        columns = pl.ds(pl.multiple_of(place * quarter, quarter), quarter)
        block = dot_f32(gate_ref[...], w_gate[:, columns], 1, 0)
        block += dot_f32(up_ref[...], w_up[:, columns], 1, 0)
        target[:slots, fold * quarter : (fold + 1) * quarter] = block.astype(bf16)


def keep_kernel(units, gate_ref, up_ref, sums_ref, *refs):
    sources = refs[:6]
    kept_ref, w_gate, w_up, sems = refs[6:]
    gate_copies = load_units(sources, 0, units, w_gate, sems)
    up_copies = load_units(sources, 1, units, w_up, sems)
    slots = gate_ref.shape[0]
    kept_ref[slots:] = sums_ref[...]
    wait_all(gate_copies)
    wait_all(up_copies)
    blocks(gate_ref, up_ref, w_gate, w_up, is_outer(), ((0, 1), (3, 2)), kept_ref, slots)


def grad_kernel(units, rows_ref, grads_ref, gate_ref, up_ref, hidden_ref, part_ref):
    pairs = ((gate_ref, rows_ref), (up_ref, rows_ref), (hidden_ref, grads_ref))
    for place, (back, source) in enumerate(pairs):
        result = dot_f32(back[...], source[...], 0, 0)
        part_ref[place * units : (place + 1) * units] = result.astype(bf16)


def total_kernel(units, kept_ref, twin_ref, far_ref, gate_ref, up_ref, down_ref):
    for place, target in enumerate((gate_ref, up_ref, down_ref)):
        part = slice(place * units, (place + 1) * units)
        target[...] = (
            kept_ref[part].astype(f32) + twin_ref[part].astype(f32) + far_ref[part].astype(f32)
        ).astype(bf16)


def give_kernel(kept_ref, got_ref, give_ref):
    slots = kept_ref.shape[0] - EXTRA
    quarter = kept_ref.shape[1] // FOLDS
    wide = give_ref.shape[0]
    experts = wide // TILE
    heads = experts * HEAD
    slot = iota(wide, heads, 1)
    target = iota(wide, heads, 0)
    rest_slot = iota(wide, experts, 1)
    rest_target = iota(wide, experts, 0)
    main = jnp.zeros((wide, quarter), f32)
    tail = jnp.zeros((wide, LANES), f32)
    for fold in range(FOLDS):
        columns = slice(fold * quarter, (fold + 1) * quarter)
        route = kept_ref[:slots, columns].astype(f32) + got_ref[:slots, columns].astype(f32)
        route = route.astype(bf16)
        pick = as_mask(target == slot // HEAD * TILE + fold * HEAD + slot % HEAD).astype(bf16)
        main += dot_f32(pick, route[:heads], 1, 0)
        for index in range(HEAD):
            pick = as_mask(rest_target == rest_slot * TILE + fold * HEAD + index).astype(bf16)
            tail += dot_f32(pick, route[heads:, index * LANES : (index + 1) * LANES], 1, 0)
    give_ref[:, :quarter] = main.astype(bf16)
    give_ref[:, quarter : quarter + LANES] = tail.astype(bf16)
    both = kept_ref[slots:, :slots].astype(f32) + got_ref[slots:, :slots].astype(f32)
    total = jnp.sum(both, axis=0, keepdims=True)
    high = total.astype(bf16).astype(f32)
    rows = iota(LANES, slots, 0)
    spread = jnp.where(rows == 0, high, jnp.where(rows == 1, total - high, 0.0)).astype(bf16)
    place = iota(wide, slots, 0)
    column = iota(wide, slots, 1)
    row = place % TILE
    expected = jnp.where(row < HEAD, place // TILE * HEAD + row, heads + place // TILE)
    pick = as_mask((column == expected) & (row < SHARE)).astype(bf16)
    give_ref[:, quarter + LANES :] = dot_f32(pick, spread, 1, 1).astype(bf16)


def combine_kernel(ids_ref, back_ref, own_ref, pass_ref):
    ids = ids_ref[...]
    tokens = ids.shape[0]
    quarter = own_ref.shape[1]
    wide = back_ref.shape[0]
    experts = wide // TILE
    upper = is_upper()
    code = place_codes(ids, experts, upper)
    spread = as_mask(iota(experts, wide, 0) == iota(experts, wide, 1) // TILE).astype(bf16)
    wide_code = dot_f32(code.astype(bf16), spread, 1, 0)
    row = iota(tokens, wide, 1) % TILE
    head = wide_code == (row % HEAD).astype(f32)
    rest = wide_code == float(HEAD)
    back_main = back_ref[:, :quarter]
    back_tail = back_ref[:, quarter : quarter + LANES]
    sums = []
    for fold in range(FOLDS):
        pick = as_mask(head & (row // HEAD == fold)).astype(bf16)
        tails = []
        for index in range(HEAD):
            tail_pick = as_mask(rest & (row == fold * HEAD + index)).astype(bf16)
            tails.append(dot_f32(tail_pick, back_tail, 1, 0))
        sums.append(dot_f32(pick, back_main, 1, 0) + jnp.concatenate(tails, axis=1))
    own_ref[...] = jnp.where(upper, sums[1], sums[0])
    pass_ref[:, :quarter] = jnp.where(upper, sums[0], sums[1]).astype(bf16)
    columns = back_ref[:, quarter + LANES :].astype(f32)
    lane = iota(wide, LANES, 1)
    expert = iota(wide, LANES, 0) // TILE
    by_lane = jnp.where(lane == expert, columns[:, 0:1], 0.0)
    by_lane += jnp.where(lane == expert + LANES // 2, columns[:, 1:2], 0.0)
    pick = as_mask(wide_code == row.astype(f32)).astype(bf16)
    pass_ref[:, quarter:] = dot_f32(pick, by_lane.astype(bf16), 1, 0).astype(bf16)


def finish_kernel(ids_ref, probs_ref, own_ref, pass_ref, got_ref, input_ref, prob_ref):
    ids = ids_ref[...]
    tokens, top_count = ids.shape
    quarter = own_ref.shape[1]
    input_ref[...] = (own_ref[...] + got_ref[:, :quarter].astype(f32)).astype(bf16)
    total = pass_ref[:, quarter:].astype(f32) + got_ref[:, quarter:].astype(f32)
    expert = iota(tokens, LANES, 1) % (LANES // 2)
    ones = jnp.ones((TILE, LANES), bf16)
    for top in range(top_count):
        chosen = jnp.where(ids[:, top : top + 1] == expert, total, 0.0).astype(bf16)
        sums = dot_f32(ones, chosen, 1, 1)[:1]
        prob_ref[top : top + 1] = sums / probs_ref[top : top + 1].astype(f32)


def shards(activations, cotangent, expert_ids, route_probs, gate_weight, up_weight, down_weight):
    tokens, quarter = activations.shape
    experts = lax.axis_size("ep") // 2
    units = gate_weight.shape[1]
    wide = experts * TILE
    slots = experts * SHARE
    edge = quarter + LANES

    got_tokens = row_partner(jnp.concatenate([activations, cotangent], axis=0))
    own_weights = jnp.concatenate([gate_weight[0], up_weight[0], down_weight[0]], axis=0)
    got_tokens, own_weights = lax.optimization_barrier((got_tokens, own_weights))
    far_weights = row_partner(own_weights)
    own_twin = other_core(own_weights)
    send = local_call(
        pack_kernel,
        shape(wide, 2 * edge, bf16),
        expert_ids,
        route_probs,
        activations,
        cotangent,
        got_tokens,
    )
    got = exchange_chips(send.reshape(experts, TILE, 2 * edge)).reshape(wide, 2 * edge)
    theirs = unit_partner(got)
    far_twin = [other_core(far_weights[i * units : (i + 1) * units]) for i in range(3)]
    sources = (far_weights, *far_twin, own_weights, own_twin)

    vmem = pl.BlockSpec(memory_space=pltpu.VMEM)
    stay = pl.BlockSpec(memory_space=pl.ANY)
    model = 4 * quarter
    unit_rows = pltpu.VMEM((4 * units, model), bf16)
    full = shape(slots, model, bf16)
    back = shape(slots, 4 * units, bf16)
    part = shape(slots, units, bf16)
    full_rows, full_grads, gate_back, up_back, sums, given, *parts = local_call(
        functools.partial(back_kernel, units),
        (full, full, back, back)
        + (shape(EXTRA, 2 * quarter, bf16), shape(slots + EXTRA, 2 * quarter, bf16))
        + (part,) * 12,
        got,
        theirs,
        *sources,
        mib=30,
        in_specs=[vmem] * 2 + [stay] * 6,
        out_specs=(vmem,) * 18,
        scratch_shapes=[unit_rows] * 3 + [pltpu.SemaphoreType.DMA((12,))],
    )
    taken = unit_partner(given)

    def set_grads(place):
        return local_call(
            functools.partial(grad_kernel, units),
            shape(3 * units, model, bf16),
            full_rows,
            full_grads,
            *parts[3 * place : 3 * place + 3],
            mib=16,
        )

    far_taken = other_core(set_grads(1))
    far_grads = (set_grads(0).astype(f32) + far_taken.astype(f32)).astype(bf16)
    far_got = row_partner(far_grads)
    near_taken = other_core(set_grads(3))
    near_kept = set_grads(2)
    kept = local_call(
        functools.partial(keep_kernel, units),
        shape(slots + EXTRA, 2 * quarter, bf16),
        gate_back,
        up_back,
        sums,
        *sources,
        mib=18,
        in_specs=[vmem] * 3 + [stay] * 6,
        out_specs=vmem,
        scratch_shapes=[unit_rows] * 2 + [pltpu.SemaphoreType.DMA((12,))],
    )
    taken, far_grads = lax.optimization_barrier((taken, far_grads))

    give = local_call(give_kernel, shape(wide, edge + LANES, bf16), kept, taken)
    back = exchange_chips(give.reshape(experts, TILE, edge + LANES)).reshape(wide, edge + LANES)
    own_sum, passed = local_call(
        combine_kernel,
        (shape(tokens, quarter, f32), shape(tokens, quarter + LANES, bf16)),
        expert_ids,
        back,
    )
    got_passed = row_partner(passed)
    unit_grad = shape(units, model, bf16)
    whole = pl.BlockSpec((3 * units, quarter), lambda i: (0, i))
    third = pl.BlockSpec((units, quarter), lambda i: (0, i))
    gate_grad, up_grad, down_grad = local_call(
        functools.partial(total_kernel, units),
        (unit_grad,) * 3,
        near_kept,
        near_taken,
        far_got,
        grid=(4,),
        in_specs=[whole] * 3,
        out_specs=(third,) * 3,
    )
    got_passed, gate_grad, up_grad, down_grad = lax.optimization_barrier(
        (got_passed, gate_grad, up_grad, down_grad)
    )
    input_grad, prob_grad = local_call(
        finish_kernel,
        (shape(tokens, quarter, bf16), shape(expert_ids.shape[1], tokens, f32)),
        expert_ids,
        route_probs.T,
        own_sum,
        passed,
        got_passed,
    )
    return (input_grad, prob_grad.T, gate_grad[None], up_grad[None], down_grad[None])


def solution(mesh):
    placed = (
        P("ep", "et"),
        P("ep", "et"),
        P("ep", None),
        P("ep", None),
        P("ep", "et", None),
        P("ep", "et", None),
        P("ep", "et", None),
    )
    return jax.shard_map(
        shards,
        mesh=mesh,
        in_specs=placed,
        out_specs=(
            P("ep", "et"),
            P("ep", None),
            P("ep", "et", None),
            P("ep", "et", None),
            P("ep", "et", None),
        ),
        check_vma=False,
    )
```

```python
import functools

import jax
import jax.numpy as jnp
from jax import lax
from jax.experimental import pallas as pl
from jax.experimental.pallas import tpu as pltpu
from jax.sharding import PartitionSpec as P

CAPACITY = 10
SHARE = CAPACITY // 2
HEAD = 4
TILE = 8
FOLDS = TILE // HEAD
LANES = 128
EXTRA = 16

bf16 = jnp.bfloat16
f32 = jnp.float32


def dot_f32(left, right, left_dim, right_dim):
    return lax.dot_general(
        left, right, (((left_dim,), (right_dim,)), ((), ())), preferred_element_type=f32
    )


def local_call(body, out_shape, *operands, mib=12, flops=0, **options):
    return pl.pallas_call(
        body,
        out_shape=out_shape,
        cost_estimate=pl.CostEstimate(flops=flops, bytes_accessed=0, transcendentals=0),
        compiler_params=pltpu.CompilerParams(vmem_limit_bytes=mib * 1024 * 1024),
        **options,
    )(*operands)


def shape(rows, columns, dtype):
    return jax.ShapeDtypeStruct((rows, columns), dtype)


def iota(rows, columns, dim):
    return lax.broadcasted_iota(jnp.int32, (rows, columns), dim)


def exchange_chips(block):
    devices = lax.axis_size("ep")
    return lax.all_to_all(
        block,
        "ep",
        split_axis=0,
        concat_axis=0,
        axis_index_groups=[list(range(core, devices, 2)) for core in range(2)],
        tiled=True,
    )


def other_core(value):
    pairs = [(source, source ^ 1) for source in range(lax.axis_size("ep"))]
    return lax.ppermute(value, "ep", pairs)


def row_partner(value):
    count = lax.axis_size("et")
    return lax.ppermute(value, "et", [(source, count - 1 - source) for source in range(count)])


def unit_partner(value):
    pairs = [(source, source ^ 1) for source in range(lax.axis_size("et"))]
    return lax.ppermute(value, "et", pairs)


def is_upper():
    return lax.axis_index("et") >= 2


def is_outer():
    index = lax.axis_index("et")
    return (index == 0) | (index == 3)


def hit_of(ids, top, experts):
    return ids[:, top : top + 1] == iota(ids.shape[0], experts, 1)


def place_codes(ids, experts, upper):
    tokens, top_count = ids.shape
    hit = sum(hit_of(ids, top, experts).astype(f32) for top in range(top_count))
    earlier = (iota(tokens, tokens, 1) < iota(tokens, tokens, 0)).astype(f32).astype(bf16)
    rank = dot_f32(earlier, hit.astype(bf16), 1, 0)
    shift = jnp.where(upper, float(SHARE), 0.0)
    return jnp.where(hit > 0.0, rank - shift, 255.0)


def as_mask(condition):
    return jnp.where(condition, 1.0, 0.0)


def packed(wide_code, wide_weight, fold, x, dy, target, base=None):
    wide, tokens = wide_code.shape
    quarter = x.shape[1]
    row = iota(wide, tokens, 0) % TILE
    mine = row // HEAD == fold
    head = jnp.where(mine & (wide_code == (row % HEAD).astype(f32)), 1.0, 0.0)
    rest = mine & (wide_code == float(HEAD))
    for side, (scale, source) in enumerate(((1.0, x), (wide_weight, dy))):
        start = side * (quarter + LANES)
        main = dot_f32((head * scale).astype(bf16), source, 1, 0).astype(bf16)
        tail = jnp.zeros((wide, LANES), f32)
        for index in range(HEAD):
            pick = (jnp.where(rest & (row % HEAD == index), 1.0, 0.0) * scale).astype(bf16)
            tail += dot_f32(pick, source[:, index * LANES : (index + 1) * LANES], 1, 0)
        tail = tail.astype(bf16)
        if base is not None:
            main += base[:, start : start + quarter]
            tail += base[:, start + quarter : start + quarter + LANES]
        target[:, start : start + quarter] = main
        target[:, start + quarter : start + quarter + LANES] = tail


def pack_own_kernel(ids_ref, probs_ref, x_ref, dy_ref, send_ref, code_ref, weight_ref):
    ids = ids_ref[...]
    wide = send_ref.shape[0]
    experts = wide // TILE
    upper = is_upper()
    code = place_codes(ids, experts, upper)
    probs = probs_ref[...].astype(f32)
    weight = sum(
        jnp.where(hit_of(ids, top, experts), probs[:, top : top + 1], 0.0)
        for top in range(ids.shape[1])
    )
    spread = as_mask(iota(wide, experts, 0) // TILE == iota(wide, experts, 1)).astype(bf16)
    wide_code = dot_f32(spread, code.astype(bf16), 1, 1)
    wide_weight = dot_f32(spread, weight.astype(bf16), 1, 1)
    code_ref[...] = wide_code
    weight_ref[...] = wide_weight
    packed(wide_code, wide_weight, jnp.where(upper, 1, 0), x_ref[...], dy_ref[...], send_ref)


def pack_got_kernel(code_ref, weight_ref, got_ref, base_ref, send_ref):
    tokens = code_ref.shape[1]
    fold = jnp.where(is_upper(), 0, 1)
    x, dy = got_ref[:tokens], got_ref[tokens:]
    packed(code_ref[...], weight_ref[...], fold, x, dy, send_ref, base_ref[...])


def unpack(block, fold):
    wide, quarter = block.shape[0], block.shape[1] - LANES
    experts = wide // TILE
    heads = experts * HEAD
    slot = iota(heads, wide, 0)
    source = iota(heads, wide, 1)
    pick = as_mask(source == slot // HEAD * TILE + fold * HEAD + slot % HEAD).astype(bf16)
    main = dot_f32(pick, block[:, :quarter], 1, 0)
    rest_slot = iota(experts, wide, 0)
    rest_source = iota(experts, wide, 1)
    tails = []
    for index in range(HEAD):
        pick = as_mask(rest_source == rest_slot * TILE + fold * HEAD + index).astype(bf16)
        tails.append(dot_f32(pick, block[:, quarter:], 1, 0))
    return jnp.concatenate([main, jnp.concatenate(tails, axis=1)], axis=0).astype(bf16)


def column_block(place, quarter):
    return pl.ds(pl.multiple_of(place * quarter, quarter), quarter)


def load_units(sources, kind, units, target, sems):
    far, twin, own, own_twin = sources[0], sources[1 + kind], sources[4], sources[5]
    rows = pl.ds(kind * units, units)
    pieces = (far.at[rows], twin, own.at[rows], own_twin.at[rows])
    copies = []
    for place, piece in enumerate(pieces):
        copy = pltpu.make_async_copy(
            piece, target.at[pl.ds(place * units, units)], sems.at[kind * 4 + place]
        )
        copy.start()
        copies.append(copy)
    return copies


def wait_all(copies):
    for copy in copies:
        copy.wait()


def own_kernel(got_ref, rows_ref, grads_ref):
    edge = got_ref.shape[1] // 2
    quarter = edge - LANES
    for fold in range(FOLDS):
        columns = slice(fold * quarter, (fold + 1) * quarter)
        rows_ref[:, columns] = unpack(got_ref[:, :edge], fold)
        grads_ref[:, columns] = unpack(got_ref[:, edge:], fold)


def back_kernel(units, got_ref, own_rows, own_grads, *refs):
    sources = refs[:6]
    rows_ref, grads_ref, gate_ref, up_ref, sums_ref, given_ref = refs[6:12]
    parts = refs[12:24]
    w_gate, w_up, w_down, sems = refs[24:]
    gate_copies = load_units(sources, 0, units, w_gate, sems)
    up_copies = load_units(sources, 1, units, w_up, sems)
    down_copies = load_units(sources, 2, units, w_down, sems)
    outer = is_outer()
    slots = rows_ref.shape[0]
    quarter = rows_ref.shape[1] // 4
    edge = quarter + LANES

    def fill(target, own, block):
        for fold, (outer_place, inner_place) in enumerate(((0, 1), (3, 2))):
            mine = column_block(jnp.where(outer, outer_place, inner_place), quarter)
            theirs = column_block(jnp.where(outer, inner_place, outer_place), quarter)
            target[:, mine] = own[:, fold * quarter : (fold + 1) * quarter]
            target[:, theirs] = unpack(block, fold)

    fill(rows_ref, own_rows, got_ref[:, :edge])
    wait_all(gate_copies)
    pre_gate = dot_f32(rows_ref[...], w_gate[...], 1, 1)
    wait_all(up_copies)
    pre_up = dot_f32(rows_ref[...], w_up[...], 1, 1)
    fill(grads_ref, own_grads, got_ref[:, edge:])
    wait_all(down_copies)
    down_back = dot_f32(grads_ref[...], w_down[...], 1, 1)
    sigmoid = jax.nn.sigmoid(pre_gate)
    silu_value = pre_gate * sigmoid
    hidden = silu_value * pre_up
    slope = sigmoid * (1.0 + pre_gate * (1.0 - sigmoid))
    gate_back = (down_back * pre_up * slope).astype(bf16)
    up_back = (down_back * silu_value).astype(bf16)
    hidden_bf = hidden.astype(bf16)
    gate_ref[...] = gate_back
    up_ref[...] = up_back
    for kind, value in enumerate((gate_back, up_back, hidden_bf)):
        for place in range(4):
            parts[3 * place + kind][...] = value[:, place * units : (place + 1) * units]
    product = hidden * down_back
    high = product.astype(bf16)
    low = (product - high.astype(f32)).astype(bf16)
    ones = jnp.ones((EXTRA, product.shape[1]), bf16)
    total = dot_f32(ones, high, 1, 1) + dot_f32(ones, low, 1, 1)
    high = total.astype(bf16).astype(f32)
    row = iota(EXTRA, slots, 0)
    sums = jnp.where(row == 0, high, jnp.where(row == 1, total - high, 0.0)).astype(bf16)
    sums_ref[...] = jnp.zeros_like(sums_ref)
    sums_ref[:, :slots] = sums
    given_ref[slots:, :] = jnp.zeros((EXTRA, given_ref.shape[1]), bf16)
    given_ref[slots:, :slots] = sums
    blocks(gate_ref, up_ref, w_gate, w_up, outer, ((1, 0), (2, 3)), given_ref, slots)


def blocks(gate_ref, up_ref, w_gate, w_up, outer, places, target, slots):
    quarter = target.shape[1] // FOLDS
    for fold, (outer_place, inner_place) in enumerate(places):
        columns = column_block(jnp.where(outer, outer_place, inner_place), quarter)
        block = dot_f32(gate_ref[...], w_gate[:, columns], 1, 0)
        block += dot_f32(up_ref[...], w_up[:, columns], 1, 0)
        target[:slots, fold * quarter : (fold + 1) * quarter] = block.astype(bf16)


def keep_kernel(units, gate_ref, up_ref, sums_ref, *refs):
    sources = refs[:6]
    kept_ref, w_gate, w_up, sems = refs[6:]
    gate_copies = load_units(sources, 0, units, w_gate, sems)
    up_copies = load_units(sources, 1, units, w_up, sems)
    slots = gate_ref.shape[0]
    kept_ref[slots:] = sums_ref[...]
    wait_all(gate_copies)
    wait_all(up_copies)
    blocks(gate_ref, up_ref, w_gate, w_up, is_outer(), ((0, 1), (3, 2)), kept_ref, slots)


def grad_kernel(rows_ref, grads_ref, gate_ref, up_ref, hidden_ref, *part_refs):
    pairs = ((gate_ref, rows_ref), (up_ref, rows_ref), (hidden_ref, grads_ref))
    for place, (back, source) in enumerate(pairs):
        result = dot_f32(back[...], source[...], 0, 0).astype(bf16)
        units = result.shape[0]
        if len(part_refs) == 1:
            part_refs[0][place * units : (place + 1) * units] = result
        else:
            part_refs[place][...] = result


def near_kernel(units, kept_ref, gate_twin, up_twin, down_twin, near_ref):
    for place, twin in enumerate((gate_twin, up_twin, down_twin)):
        part = slice(place * units, (place + 1) * units)
        near_ref[part] = kept_ref[part] + twin[...]


def total_kernel(units, near_ref, far_ref, *refs):
    targets = refs[:3]
    far_rows, in_sems, out_sems = refs[3:]
    loads, stores = [], []
    for place in range(3):
        part = pl.ds(place * units, units)
        copy = pltpu.make_async_copy(far_ref.at[part], far_rows.at[part], in_sems.at[place])
        copy.start()
        loads.append(copy)
    for place, target in enumerate(targets):
        part = pl.ds(place * units, units)
        loads[place].wait()
        far_rows[part] = near_ref[part] + far_rows[part]
        copy = pltpu.make_async_copy(far_rows.at[part], target, out_sems.at[place])
        copy.start()
        stores.append(copy)
    wait_all(stores)


def far_kernel(
    rows_ref, grads_ref, gate_ref, up_ref, hidden_ref, taken_ref, part_ref, taken_rows, sem
):
    copy = pltpu.make_async_copy(taken_ref, taken_rows, sem.at[0])
    copy.start()
    pairs = ((gate_ref, rows_ref), (up_ref, rows_ref), (hidden_ref, grads_ref))
    for place, (back, source) in enumerate(pairs):
        result = dot_f32(back[...], source[...], 0, 0)
        if place == 0:
            copy.wait()
        units = result.shape[0]
        part = slice(place * units, (place + 1) * units)
        part_ref[part] = (result + taken_rows[part].astype(f32)).astype(bf16)


def give_kernel(kept_ref, got_ref, give_ref):
    slots = kept_ref.shape[0] - EXTRA
    quarter = kept_ref.shape[1] // FOLDS
    wide = give_ref.shape[0]
    experts = wide // TILE
    heads = experts * HEAD
    slot = iota(wide, heads, 1)
    target = iota(wide, heads, 0)
    rest_slot = iota(wide, experts, 1)
    rest_target = iota(wide, experts, 0)
    main = jnp.zeros((wide, quarter), f32)
    tail = jnp.zeros((wide, LANES), f32)
    for fold in range(FOLDS):
        columns = slice(fold * quarter, (fold + 1) * quarter)
        route = kept_ref[:slots, columns].astype(f32) + got_ref[:slots, columns].astype(f32)
        route = route.astype(bf16)
        pick = as_mask(target == slot // HEAD * TILE + fold * HEAD + slot % HEAD).astype(bf16)
        main += dot_f32(pick, route[:heads], 1, 0)
        for index in range(HEAD):
            pick = as_mask(rest_target == rest_slot * TILE + fold * HEAD + index).astype(bf16)
            tail += dot_f32(pick, route[heads:, index * LANES : (index + 1) * LANES], 1, 0)
    give_ref[:, :quarter] = main.astype(bf16)
    give_ref[:, quarter : quarter + LANES] = tail.astype(bf16)
    both = kept_ref[slots:, :slots].astype(f32) + got_ref[slots:, :slots].astype(f32)
    total = jnp.sum(both, axis=0, keepdims=True)
    high = total.astype(bf16).astype(f32)
    rows = iota(LANES, slots, 0)
    spread = jnp.where(rows == 0, high, jnp.where(rows == 1, total - high, 0.0)).astype(bf16)
    place = iota(wide, slots, 0)
    column = iota(wide, slots, 1)
    row = place % TILE
    expected = jnp.where(row < HEAD, place // TILE * HEAD + row, heads + place // TILE)
    pick = as_mask((column == expected) & (row < SHARE)).astype(bf16)
    give_ref[:, quarter + LANES :] = dot_f32(pick, spread, 1, 1).astype(bf16)


def combine_kernel(ids_ref, back_ref, own_ref, pass_ref):
    ids = ids_ref[...]
    tokens = ids.shape[0]
    quarter = own_ref.shape[1]
    wide = back_ref.shape[0]
    experts = wide // TILE
    upper = is_upper()
    code = place_codes(ids, experts, upper)
    spread = as_mask(iota(experts, wide, 0) == iota(experts, wide, 1) // TILE).astype(bf16)
    wide_code = dot_f32(code.astype(bf16), spread, 1, 0)
    row = iota(tokens, wide, 1) % TILE
    head = wide_code == (row % HEAD).astype(f32)
    rest = wide_code == float(HEAD)
    back_main = back_ref[:, :quarter]
    back_tail = back_ref[:, quarter : quarter + LANES]
    sums = []
    for fold in range(FOLDS):
        pick = as_mask(head & (row // HEAD == fold)).astype(bf16)
        tails = []
        for index in range(HEAD):
            tail_pick = as_mask(rest & (row == fold * HEAD + index)).astype(bf16)
            tails.append(dot_f32(tail_pick, back_tail, 1, 0))
        sums.append(dot_f32(pick, back_main, 1, 0) + jnp.concatenate(tails, axis=1))
    own_ref[...] = jnp.where(upper, sums[1], sums[0])
    pass_ref[:, :quarter] = jnp.where(upper, sums[0], sums[1]).astype(bf16)
    columns = back_ref[:, quarter + LANES :].astype(f32)
    lane = iota(wide, LANES, 1)
    expert = iota(wide, LANES, 0) // TILE
    by_lane = jnp.where(lane == expert, columns[:, 0:1], 0.0)
    by_lane += jnp.where(lane == expert + LANES // 2, columns[:, 1:2], 0.0)
    pick = as_mask(wide_code == row.astype(f32)).astype(bf16)
    pass_ref[:, quarter:] = dot_f32(pick, by_lane.astype(bf16), 1, 0).astype(bf16)


def finish_kernel(ids_ref, probs_ref, own_ref, pass_ref, got_ref, input_ref, prob_ref):
    ids = ids_ref[...]
    tokens, top_count = ids.shape
    quarter = own_ref.shape[1]
    input_ref[...] = (own_ref[...] + got_ref[:, :quarter].astype(f32)).astype(bf16)
    total = pass_ref[:, quarter:].astype(f32) + got_ref[:, quarter:].astype(f32)
    expert = iota(tokens, LANES, 1) % (LANES // 2)
    ones = jnp.ones((TILE, LANES), bf16)
    for top in range(top_count):
        chosen = jnp.where(ids[:, top : top + 1] == expert, total, 0.0).astype(bf16)
        sums = dot_f32(ones, chosen, 1, 1)[:1]
        prob_ref[top : top + 1] = sums / probs_ref[top : top + 1].astype(f32)


def shards(activations, cotangent, expert_ids, route_probs, gate_weight, up_weight, down_weight):
    tokens, quarter = activations.shape
    experts = lax.axis_size("ep") // 2
    units = gate_weight.shape[1]
    wide = experts * TILE
    slots = experts * SHARE
    edge = quarter + LANES

    got_tokens = row_partner(jnp.concatenate([activations, cotangent], axis=0))
    own_weights = jnp.concatenate([gate_weight[0], up_weight[0], down_weight[0]], axis=0)
    got_tokens, own_weights = lax.optimization_barrier((got_tokens, own_weights))
    far_weights = row_partner(own_weights)
    own_twin = other_core(own_weights)
    send_shape = shape(wide, 2 * edge, bf16)
    base, code, weight = local_call(
        pack_own_kernel,
        (send_shape, shape(wide, tokens, f32), shape(wide, tokens, f32)),
        expert_ids,
        route_probs,
        activations,
        cotangent,
    )
    send = local_call(pack_got_kernel, send_shape, code, weight, got_tokens, base)
    got = exchange_chips(send.reshape(experts, TILE, 2 * edge)).reshape(wide, 2 * edge)
    theirs = unit_partner(got)
    far_twin = [other_core(far_weights[i * units : (i + 1) * units]) for i in range(3)]
    sources = (far_weights, *far_twin, own_weights, own_twin)

    vmem = pl.BlockSpec(memory_space=pltpu.VMEM)
    stay = pl.BlockSpec(memory_space=pl.ANY)
    far = pl.BlockSpec(memory_space=pltpu.HBM)
    model = 4 * quarter
    unit_rows = pltpu.VMEM((4 * units, model), bf16)
    full = shape(slots, model, bf16)
    back = shape(slots, 4 * units, bf16)
    part = shape(slots, units, bf16)
    own_half = shape(slots, 2 * quarter, bf16)
    halves = local_call(own_kernel, (own_half,) * 2, got)
    full_rows, full_grads, gate_back, up_back, sums, given, *parts = local_call(
        functools.partial(back_kernel, units),
        (full, full, back, back)
        + (shape(EXTRA, 2 * quarter, bf16), shape(slots + EXTRA, 2 * quarter, bf16))
        + (part,) * 12,
        theirs,
        *halves,
        *sources,
        mib=30,
        in_specs=[vmem] * 3 + [stay] * 6,
        out_specs=(vmem,) * 18,
        scratch_shapes=[unit_rows] * 3 + [pltpu.SemaphoreType.DMA((12,))],
    )
    taken = unit_partner(given)

    def set_grads(out, *backs):
        return local_call(grad_kernel, out, full_rows, full_grads, *backs, mib=16)

    whole_part = shape(3 * units, model, bf16)
    unit_grad = shape(units, model, bf16)
    far_taken = other_core(set_grads(whole_part, *parts[3:6]))
    far_grads = local_call(
        far_kernel,
        whole_part,
        full_rows,
        full_grads,
        *parts[:3],
        far_taken,
        mib=16,
        in_specs=[vmem] * 5 + [stay],
        out_specs=vmem,
        scratch_shapes=[
            pltpu.VMEM((3 * units, model), bf16),
            pltpu.SemaphoreType.DMA((1,)),
        ],
    )
    far_got = row_partner(far_grads)
    far_grads, *near = lax.optimization_barrier((far_grads, *parts[6:]))
    near_taken = [other_core(part) for part in set_grads((unit_grad,) * 3, *near[3:])]
    near_kept = set_grads(whole_part, *near[:3])
    kept = local_call(
        functools.partial(keep_kernel, units),
        shape(slots + EXTRA, 2 * quarter, bf16),
        gate_back,
        up_back,
        sums,
        *sources,
        mib=18,
        in_specs=[vmem] * 3 + [stay] * 6,
        out_specs=vmem,
        scratch_shapes=[unit_rows] * 2 + [pltpu.SemaphoreType.DMA((12,))],
    )
    taken, far_grads = lax.optimization_barrier((taken, far_grads))

    give = local_call(give_kernel, shape(wide, edge + LANES, bf16), kept, taken)
    back = exchange_chips(give.reshape(experts, TILE, edge + LANES)).reshape(wide, edge + LANES)
    near_sum = local_call(
        functools.partial(near_kernel, units), whole_part, near_kept, *near_taken
    )
    back, near_sum = lax.optimization_barrier((back, near_sum))
    own_sum, passed = local_call(
        combine_kernel,
        (shape(tokens, quarter, f32), shape(tokens, quarter + LANES, bf16)),
        expert_ids,
        back,
    )
    got_passed = row_partner(passed)
    rows_scratch = pltpu.VMEM((3 * units, model), bf16)
    gate_grad, up_grad, down_grad = local_call(
        functools.partial(total_kernel, units),
        (unit_grad,) * 3,
        near_sum,
        far_got,
        in_specs=[vmem, far],
        out_specs=(stay,) * 3,
        scratch_shapes=[
            rows_scratch,
            pltpu.SemaphoreType.DMA((3,)),
            pltpu.SemaphoreType.DMA((3,)),
        ],
    )
    got_passed, gate_grad, up_grad, down_grad = lax.optimization_barrier(
        (got_passed, gate_grad, up_grad, down_grad)
    )
    input_grad, prob_grad = local_call(
        finish_kernel,
        (shape(tokens, quarter, bf16), shape(expert_ids.shape[1], tokens, f32)),
        expert_ids,
        route_probs.T,
        own_sum,
        passed,
        got_passed,
    )
    return (input_grad, prob_grad.T, gate_grad[None], up_grad[None], down_grad[None])


def solution(mesh):
    placed = (
        P("ep", "et"),
        P("ep", "et"),
        P("ep", None),
        P("ep", None),
        P("ep", "et", None),
        P("ep", "et", None),
        P("ep", "et", None),
    )
    return jax.shard_map(
        shards,
        mesh=mesh,
        in_specs=placed,
        out_specs=(
            P("ep", "et"),
            P("ep", None),
            P("ep", "et", None),
            P("ep", "et", None),
            P("ep", "et", None),
        ),
        check_vma=False,
    )
```
